256 devices in a mesh: dp: 16 (over x_lo, y, core), expert: 16 (over x_hi, z).
Axes of the slice: x: 4 (x_hi: 2, x_lo: 2; x = x_hi * 2 + x_lo), y: 4, z: 8, core: 2. Of those that a mesh axis runs over, the one named last changes fastest.
Arguments:
- out_grad: bfloat16 [32768, 5120], P(('dp', 'expert')), may hold values from -6 to 6
- expert_ids: int32 [32768, 1], P(('dp', 'expert')), may hold values from 0 to 15; in each aligned block of 128 rows (0 to 127, 128 to 255, ...) at most 10 rows name the same one
- router_logit: float32 [32768], P(('dp', 'expert')), may hold values from -8 to 8
- hidden_saved: bfloat16 [16, 2560, 4096], P('expert', None, 'dp'), may hold values from -60 to 60
- down_weight: bfloat16 [16, 4096, 5120], P('expert', 'dp'), may hold values from -0.09375 to 0.09375
Outputs:
- weight_grad: bfloat16 [16, 4096, 5120], P('expert', 'dp')
- logit_grad: float32 [32768], P(('dp', 'expert'))
The draws below stay inside these ranges and needn't reach their ends.
Inputs may be any that keep to these rules, and one draw needn't show every extreme that they name: `expert_ids`: within the 128 rows of one device no expert is named more than 10 times; some expert is named exactly 10 times there in every draw.
All inputs are finite; a program needn't handle non-finite values.
Results may differ from the reference program's by a relative error of at most 0.0055.
Values may be sent and summed in bfloat16 or wider, within the bound.
No kernel may reach another device: no remote copies, remote signals or barrier semaphores. Data moves between devices by JAX's collectives and lax.ppermute only.
A program may use at most 128 MiB of HBM per device.

```python
import math
import jax
import jax.numpy as jnp
import numpy as np
from jax import lax

D = 5120
F = 4096
TOK_DEV = 128
EXPERTS = 16
CAP = 10
SLOTS = 2560
TOKENS = 32768


def draw_hidden_saved(key, part):
    key = jax.random.fold_in(key, 11)
    first, second = jax.random.split(key, 2)
    spread = jnp.arange(F, dtype=jnp.float32) / (F - 1)
    column = jnp.exp(spread * math.log(3.0)) * jax.random.uniform(second, (F,), jnp.float32, 0.5, 1.5)
    base = jax.random.normal(first, (EXPERTS, SLOTS, F), jnp.float32)
    return jnp.clip(base * column, -60.0, 60.0).astype(jnp.bfloat16)


def steps_of(key, dims, cuts, smallest, top_value):
    def one(dim, blocks):
        draws = jax.random.uniform(jax.random.fold_in(jax.random.fold_in(key, 6), dim), (blocks,), jnp.float32, smallest / len(cuts), top_value / len(cuts))
        return jnp.repeat(jnp.exp(draws), dims[dim] // blocks).reshape((-1,) + (1,) * (len(dims) - dim - 1))

    loudness = one(*cuts[0])
    for cut in cuts[1:]:
        loudness = loudness * one(*cut)
    return loudness


def assign_block(own_key, own, number, rows, amount, top, bound, lean):
    sequence = jax.random.permutation(own_key, amount)
    packed, ordinary = shares(amount, rows * top, bound, lean, True), shares(amount, rows * top, bound, lean, False)
    places = jnp.arange(amount)

    def named(lengths, rotation):
        used = int((lengths > 0).sum())
        fixed = max(1, used // 4)
        passed = fixed + (places - fixed + rotation * (used - fixed)) % max(1, amount - fixed)
        return jnp.zeros((amount,), jnp.int32).at[sequence[jnp.where(places < fixed, places, passed)]].set(jnp.asarray(lengths, jnp.int32))

    lengths = jnp.where(number % 4 == 0, named(packed, number // 4), named(ordinary, number - number // 4 - 1))
    mixed = jax.random.permutation(jax.random.fold_in(own, 3), amount)
    source_of, receiver = mixed[0:amount // 2 * 2:2], mixed[1:amount // 2 * 2:2]
    room = jnp.minimum(lengths[source_of] - 1, bound - lengths[receiver]) // 2
    room = jnp.where((source_of == sequence[0]) | (receiver == sequence[0]) | (lengths[receiver] == 0), 0, jnp.maximum(room, 0))
    passed = jax.random.randint(jax.random.fold_in(own, 4), (amount // 2,), 0, 1 << 20) % (room + 1)
    lengths = lengths.at[source_of].add(-passed).at[receiver].add(passed)
    items = jnp.searchsorted(jnp.cumsum(lengths), jnp.arange(rows * top), side="right").astype(jnp.int32)
    grid = items.reshape(top, rows).T
    grid = grid[jax.random.permutation(jax.random.fold_in(own, 1), rows)]
    rotation = jax.random.randint(jax.random.fold_in(own, 2), (rows, 1), 0, top)
    return jnp.take_along_axis(grid, (jnp.arange(top)[None, :] + rotation) % top, axis=1)


def shares(count, total, limit, lean, full):
    portions = [(1 << 20) // math.isqrt(standing ** lean) + 1 for standing in range(1, count + 1)]
    largest = limit if full else min(limit, max(-(-total // count), total * portions[0] // sum(portions)))
    least = 1 if total - largest >= count - 1 else 0
    counts, rest = [largest] + [least] * (count - 1), total - largest - least * (count - 1)
    while rest > 0:
        candidates = [i for i in range(1, count) if counts[i] < largest] or [i for i in range(1, count) if counts[i] < limit]
        pool, remaining = sum([portions[i] for i in candidates]), rest
        for i in candidates:
            more = min(limit - counts[i], max(1, remaining * portions[i] // pool), rest)
            counts[i] = counts[i] + more
            rest = rest - more
    return np.array(counts)


def normal_values(key, shape, deviation, limit, shards=(), held_as=jnp.bfloat16):
    array = deviation * jax.random.normal(key, shape, jnp.float32)
    if shards:
        array = array * steps_of(key, shape, shards, -0.22, 0.18)
    return jnp.clip(array, -limit, limit).astype(held_as)


def setup_inputs(seed: int = 0) -> dict:
    splits = jax.random.split(jax.random.key(seed), 6)
    out_grad = normal_values(splits[0], (TOKENS, D), 1.0, 6.0, ((0, 256),))
    expert_ids_keys = jax.random.split(jax.random.fold_in(splits[1], 1), TOKENS // TOK_DEV)
    expert_ids_turns = jax.random.permutation(jax.random.fold_in(splits[1], 3), TOKENS // TOK_DEV)
    expert_ids = jax.vmap(lambda own, number: assign_block(jax.random.fold_in(splits[1], 2), own, number, TOK_DEV, EXPERTS, 1, CAP, 2))(expert_ids_keys, expert_ids_turns).reshape((TOKENS, 1))
    router_logit = normal_values(splits[2], (TOKENS,), 2.0, 8.0, ((0, 256),), jnp.float32)
    hidden_saved = draw_hidden_saved(jax.random.fold_in(splits[5], 71), 0)
    down_weight = normal_values(splits[4], (EXPERTS, F, D), F ** -0.5, 0.09375, ((0, 16), (1, 16)))
    return {"out_grad": out_grad, "expert_ids": expert_ids, "router_logit": router_logit, "hidden_saved": hidden_saved, "down_weight": down_weight}


def reference(out_grad, expert_ids, router_logit, hidden_saved, down_weight):
    route_ids = expert_ids[:, 0]
    tokens = route_ids.shape[0]
    experts = down_weight.shape[0]
    slot_count = hidden_saved.shape[1]
    per_block = route_ids.reshape(-1, TOK_DEV)
    onehot = (per_block[:, :, None] == jnp.arange(experts, dtype=jnp.int32)[None, None, :]).astype(jnp.int32)
    before = jnp.cumsum(onehot, axis=1) - onehot
    rank_pos = jnp.sum(before * onehot, axis=2).reshape(-1)
    owner = jnp.arange(tokens, dtype=jnp.int32) // TOK_DEV
    slot_index = (owner * CAP + rank_pos).astype(jnp.int32)
    route_prob = jax.nn.sigmoid(router_logit)
    prob_wire = route_prob.astype(jnp.bfloat16)

    def per_expert(expert):
        targets = jnp.where(route_ids == expert, slot_index, slot_count).astype(jnp.int32)
        slot_rows = jnp.zeros((slot_count, D), jnp.bfloat16).at[targets].set(out_grad, mode="drop")
        slot_probs = jnp.zeros((slot_count,), jnp.bfloat16).at[targets].set(prob_wire, mode="drop")
        saved_wide = hidden_saved[expert].astype(jnp.float32)
        scaled = (slot_probs.astype(jnp.float32)[:, None] * saved_wide).astype(jnp.bfloat16)
        weight_term = lax.dot_general(scaled, slot_rows, (((0,), (0,)), ((), ())), preferred_element_type=jnp.float32)
        back_proj = lax.dot_general(slot_rows, down_weight[expert], (((1,), (1,)), ((), ())), preferred_element_type=jnp.float32)
        scores = jnp.sum(saved_wide * back_proj, axis=1)
        return weight_term.astype(jnp.bfloat16), scores

    weight_grad, scores = lax.map(per_expert, jnp.arange(experts, dtype=jnp.int32))
    picked = scores[route_ids, slot_index]
    return weight_grad, route_prob * (1.0 - route_prob) * picked
```

```python
import jax
import jax.numpy as jnp
import numpy as np
from jax import lax
from jax.experimental import pallas as pl
from jax.experimental.pallas import tpu as pltpu
from jax.sharding import Mesh, PartitionSpec as P

BF = jnp.bfloat16
F32 = jnp.float32
CAP = 10
TOK = 128
CHUNKS = (1024, 1024, 512)
HALF = 2560
FD = 256
BLOCK = 320
SLOTS = 2560
MIB = 1 << 20
AXES = ("x_lo", "y", "core", "x_hi", "z")
VMEM = pl.BlockSpec(memory_space=pltpu.VMEM)
SMEM = pl.BlockSpec(memory_space=pltpu.SMEM)
ANY = pl.BlockSpec(memory_space=pl.ANY)


def pair_targets(own):
    i = np.arange(2 * BLOCK)
    x_lo, core, x_hi, z, r = i // 320, i // 160 % 2, i // 80 % 2, i // 10 % 8, i % 10
    return ((x_lo ^ x_hi ^ own) * 320 + z * 40 + core * 20 + x_hi * 10 + r).astype(np.int32)


def route_kernel(ids_ref, logit_ref, out_ref):
    ids = ids_ref[...].astype(F32)
    row = lax.broadcasted_iota(jnp.int32, (TOK, TOK), 0)
    col = lax.broadcasted_iota(jnp.int32, (TOK, TOK), 1)
    ids_row = jnp.sum(jnp.where(row == col, ids, 0.0), axis=0, keepdims=True)
    rank = jnp.sum(jnp.where((ids == ids_row) & (row < col), 1.0, 0.0), axis=0, keepdims=True)
    prob = jax.nn.sigmoid(logit_ref[...]).astype(BF).astype(F32)
    out_ref[...] = jnp.concatenate([ids_row, rank, prob, jnp.zeros((5, TOK), F32)], axis=0)


def route(ids, logit):
    return pl.pallas_call(
        route_kernel,
        out_shape=jax.ShapeDtypeStruct((8, TOK), F32),
        in_specs=[VMEM, VMEM],
        out_specs=VMEM,
        name="route",
    )(ids, logit.reshape(1, TOK))


def place_kernel(where_ref, m0, m1, m2, m3, t0, t1, t2, t3, out_ref):
    core, x_hi = where_ref[0], where_ref[1]
    slot = lax.broadcasted_iota(jnp.int32, (BLOCK, TOK), 0).astype(F32)
    first = (8 * x_hi).astype(F32)
    total = None
    for meta, tok, other_core, other_x in ((m0, t0, 0, 0), (m1, t1, 1, 0), (m2, t2, 0, 1), (m3, t3, 1, 1)):
        src_core = core if other_core == 0 else 1 - core
        src_x = x_hi if other_x == 0 else 1 - x_hi
        base = (src_core * 20 + src_x * 10).astype(F32)
        z = meta[0:1, :] - first
        pos = jnp.where((z >= 0.0) & (z < 8.0), z * 40.0 + meta[1:2, :] + base, -1.0)
        hot = jnp.where(slot == pos, meta[2:3, :], 0.0).astype(BF)
        part = jnp.dot(hot, tok[...], preferred_element_type=F32)
        total = part if total is None else total + part
    out_ref[...] = total.astype(BF)


def place(where, metas, toks):
    width = toks[0].shape[1]
    return pl.pallas_call(
        place_kernel,
        out_shape=jax.ShapeDtypeStruct((BLOCK, width), BF),
        in_specs=[SMEM] + [VMEM] * 8,
        out_specs=VMEM,
        compiler_params=pltpu.CompilerParams(vmem_limit_bytes=24 * MIB),
        cost_estimate=pl.CostEstimate(
            flops=2 * 4 * BLOCK * TOK * width, bytes_accessed=2 * width * (4 * TOK + BLOCK), transcendentals=0
        ),
        name="place",
    )(where, *metas, *toks)


def turn_kernel(target_ref, own_ref, par_ref, out_ref, hot_ref):
    col = lax.broadcasted_iota(jnp.int32, (2 * BLOCK, 2 * BLOCK), 1)
    hot_ref[...] = jnp.where(col == target_ref[...], 1.0, 0.0).astype(BF)
    for y in range(4):
        for half, ref in enumerate((own_ref, par_ref)):
            rows = jnp.concatenate([ref[pl.ds(y * BLOCK, BLOCK), :], ref[pl.ds((4 + y) * BLOCK, BLOCK), :]], axis=0)
            turned = lax.dot_general(rows, hot_ref[...], (((0,), (0,)), ((), ())), preferred_element_type=F32)
            out_ref[pl.ds(half * FD, FD), pl.ds(y * 2 * BLOCK, 2 * BLOCK)] = turned.astype(BF)


def turn(target, own, par):
    return pl.pallas_call(
        turn_kernel,
        out_shape=jax.ShapeDtypeStruct((2 * FD, SLOTS), BF),
        in_specs=[VMEM] * 3,
        out_specs=VMEM,
        scratch_shapes=[pltpu.VMEM((2 * BLOCK, 2 * BLOCK), BF)],
        compiler_params=pltpu.CompilerParams(vmem_limit_bytes=24 * MIB),
        cost_estimate=pl.CostEstimate(flops=2 * 2 * FD * SLOTS * 2 * BLOCK, bytes_accessed=5 * MIB, transcendentals=0),
        name="turn",
    )(target, own, par)


N_PIECES = 10


def expert_kernel(off, width, where_ref, *refs):
    pieces, (hid_ref, down_ref, par_ref, own_out, oth_out, score_ref, rows, hid, wts, sems) = refs[:N_PIECES], refs[N_PIECES:]
    core, y, x_lo = where_ref[0], where_ref[2], where_ref[3]
    copies = []

    def begin(src, dst):
        copy = pltpu.make_async_copy(src, dst, sems.at[len(copies)])
        copy.start()
        copies.append(copy)

    half = BLOCK // 2
    places = (
        (0, 0, 0, BLOCK),
        (0, 3, 0, BLOCK),
        (0, 1, 0, BLOCK),
        (0, 2, 0, half),
        (0, 2, half, half),
        (1, 0, 0, BLOCK),
        (1, 3, 0, BLOCK),
        (1, 1, 0, BLOCK),
        (1, 2, 0, half),
        (1, 2, half, half),
    )
    for ref, (other_x, up, skip, count) in zip(pieces, places):
        block = lax.rem(y + up, 4) * 2 + (x_lo if other_x == 0 else 1 - x_lo)
        start = pl.multiple_of(block * BLOCK + skip, 32)
        begin(ref, rows.at[pl.ds(start, count), :])
    begin(hid_ref, hid)
    start = pl.multiple_of(core * HALF + off, 128)
    begin(down_ref.at[:, pl.ds(start, width)], wts.at[pl.ds(0, FD), :])
    begin(par_ref.at[:, pl.ds(off, width)], wts.at[pl.ds(FD, FD), :])
    for copy in copies:
        copy.wait()

    tile = 512

    @pl.loop(0, SLOTS // tile)
    def _(i):
        at = pl.ds(pl.multiple_of(i * tile, tile), tile)
        back = lax.dot_general(wts[...], rows[at, :], (((1,), (1,)), ((), ())), preferred_element_type=F32)
        score_ref[:, at] = jnp.sum(back * hid[:, at].astype(F32), axis=0, keepdims=True)

    step = 256

    @pl.loop(0, width // step)
    def _(i):
        at = pl.ds(pl.multiple_of(i * step, step), step)
        grad = jnp.dot(hid[...], rows[:, at], preferred_element_type=F32).astype(BF)
        own_out[:, at] = grad[:FD]
        oth_out[:, at] = grad[FD:]


def expert_part(where, pieces, hid, down, par, off, width):
    return pl.pallas_call(
        lambda *refs: expert_kernel(off, width, *refs),
        out_shape=(
            jax.ShapeDtypeStruct((FD, width), BF),
            jax.ShapeDtypeStruct((FD, width), BF),
            jax.ShapeDtypeStruct((1, SLOTS), F32),
        ),
        in_specs=[SMEM] + [ANY] * (N_PIECES + 3),
        out_specs=(VMEM, VMEM, VMEM),
        scratch_shapes=[
            pltpu.VMEM((SLOTS, width), BF),
            pltpu.VMEM((2 * FD, SLOTS), BF),
            pltpu.VMEM((2 * FD, width), BF),
            pltpu.SemaphoreType.DMA((N_PIECES + 3,)),
        ],
        compiler_params=pltpu.CompilerParams(vmem_limit_bytes=24 * MIB),
        cost_estimate=pl.CostEstimate(
            flops=2 * 2 * 2 * FD * SLOTS * width, bytes_accessed=2 * SLOTS * (width + 2 * FD), transcendentals=0
        ),
        name="expert_part",
    )(where, *pieces, hid, down, par)


def join_kernel(n, where_ref, *refs):
    own, got, out_ref, sems = refs[:n], refs[n : 2 * n], refs[2 * n], refs[2 * n + 1]
    core = where_ref[0]
    copies = []
    for refs_of, side in ((own, core), (got, 1 - core)):
        off = 0
        for ref in refs_of:
            width = ref.shape[1]
            start = pl.multiple_of(side * HALF + off, 128)
            copy = pltpu.make_async_copy(ref, out_ref.at[:, pl.ds(start, width)], sems.at[len(copies)])
            copy.start()
            copies.append(copy)
            off += width
    for copy in copies:
        copy.wait()


def join(where, own, got):
    n = len(own)
    return pl.pallas_call(
        lambda *refs: join_kernel(n, *refs),
        out_shape=jax.ShapeDtypeStruct((FD, 2 * HALF), BF),
        in_specs=[SMEM] + [ANY] * (2 * n),
        out_specs=ANY,
        scratch_shapes=[pltpu.SemaphoreType.DMA((2 * n,))],
        name="join",
    )(where, *own, *got)


def ring(axis, shift):
    def send(array):
        size = lax.axis_size(axis)
        return lax.ppermute(array, axis, [(i, (i + shift) % size) for i in range(size)])

    return send


def swap_x(core_too):
    axes = ("x_lo", "core", "x_hi")
    flip = 7 if core_too else 5

    def send(array):
        return lax.ppermute(array, axes, [(i, i ^ flip) for i in range(8)])

    return send


def body(out_grad, expert_ids, router_logit, hidden_saved, down_weight):
    core, x_hi = lax.axis_index("core"), lax.axis_index("x_hi")
    y, x_lo = lax.axis_index("y"), lax.axis_index("x_lo")
    where = jnp.stack([core, x_hi, y, x_lo]).astype(jnp.int32)
    swap_core, swap_xx, swap_xc = ring("core", 1), swap_x(False), swap_x(True)
    up, down, cross = ring("y", 1), ring("y", 3), ring("x_lo", 1)
    first = core == 0
    hidden = hidden_saved[0]
    down_own = down_weight[0]

    offs = [sum(CHUNKS[:k]) for k in range(len(CHUNKS))]
    own_tok, oth_tok = [], []
    for off, width in zip(offs, CHUNKS):
        low, high = out_grad[:, off : off + width], out_grad[:, HALF + off : HALF + off + width]
        own_tok.append(jnp.where(first, low, high))
        oth_tok.append(jnp.where(first, high, low))
    meta = route(expert_ids, router_logit)
    metas = (meta, swap_core(meta), swap_xx(meta), swap_xc(meta))

    hidden_par = swap_core(hidden)
    down_par = swap_core(jnp.where(first, down_own[:, HALF:], down_own[:, :HALF]))
    target = jnp.where(x_hi == 0, pair_targets(0), pair_targets(1))
    hid = turn(target.reshape(2 * BLOCK, 1), hidden, hidden_par)

    own_grad, got_grad, score = [], [], None
    half = BLOCK // 2
    for k, (off, width) in enumerate(zip(offs, CHUNKS)):
        toks = (own_tok[k], swap_core(oth_tok[k]), swap_xx(own_tok[k]), swap_xc(oth_tok[k]))
        sent = place(where, metas, toks).reshape(8, 40, width)
        got = lax.all_to_all(sent, "z", split_axis=0, concat_axis=0, tiled=True)
        rows = got.reshape(BLOCK, width)
        below, above, over = up(rows), down(rows), cross(rows)
        far_0, far_1 = up(below[:half]), down(above[half:])
        over_below, over_above = up(over), down(over)
        over_far_0, over_far_1 = cross(far_0), cross(far_1)
        pieces = (rows, below, above, far_0, far_1, over, over_below, over_above, over_far_0, over_far_1)
        own, oth, part = expert_part(where, pieces, hid, down_own, down_par, off, width)
        own_grad.append(own)
        got_grad.append(swap_core(oth))
        score = part if score is None else score + part
    weight_grad = join(where, own_grad, got_grad)[None]

    hot = (target[:, None] == jnp.arange(2 * BLOCK, dtype=jnp.int32)[None, :]).astype(F32)
    turned = lax.dot_general(
        score.reshape(4, 2 * BLOCK), hot, (((1,), (1,)), ((), ())), precision=lax.Precision.HIGHEST,
        preferred_element_type=F32,
    )
    parts = turned.reshape(4, 2, 2, 160).transpose(1, 0, 2, 3).reshape(16, 160)
    mine = lax.all_to_all(parts, ("x_lo", "y", "core"), split_axis=0, concat_axis=0, tiled=True)
    own_scores = jnp.sum(mine, axis=0).reshape(16, CAP)
    back = lax.all_to_all(own_scores, ("x_hi", "z"), split_axis=0, concat_axis=0, tiled=True)
    slot = (meta[0] * CAP + meta[1]).astype(jnp.int32)
    hit = slot[:, None] == jnp.arange(16 * CAP, dtype=jnp.int32)[None, :]
    token_scores = jnp.sum(jnp.where(hit, back.reshape(1, 16 * CAP), 0.0), axis=1)
    prob = jax.nn.sigmoid(router_logit)
    logit_grad = prob * (1.0 - prob) / meta[2] * token_scores
    return weight_grad, logit_grad


def solution(mesh):
    fine = Mesh(mesh.devices.reshape(2, 4, 2, 2, 8), AXES)
    dp, expert = ("x_lo", "y", "core"), ("x_hi", "z")
    placed = (
        P(AXES, None),
        P(AXES, None),
        P(AXES),
        P(expert, None, dp),
        P(expert, dp, None),
    )
    return jax.shard_map(
        body,
        mesh=fine,
        in_specs=placed,
        out_specs=(P(expert, dp, None), P(AXES)),
        check_vma=False,
    )
```

```python
import jax
import jax.numpy as jnp
import numpy as np
from jax import lax
from jax.experimental import pallas as pl
from jax.experimental.pallas import tpu as pltpu
from jax.sharding import Mesh, PartitionSpec as P

BF = jnp.bfloat16
F32 = jnp.float32
CAP = 10
TOK = 128
CHUNKS = (1280, 1280)
HALF = 2560
FD = 256
BLOCK = 320
QUARTER = 1280
TOP = 160
SLOTS = 2560
MIB = 1 << 20
AXES = ("x_lo", "y", "core", "x_hi", "z")
VMEM = pl.BlockSpec(memory_space=pltpu.VMEM)
SMEM = pl.BlockSpec(memory_space=pltpu.SMEM)
ANY = pl.BlockSpec(memory_space=pl.ANY)


def pair_targets():
    i = np.arange(2 * BLOCK)
    y, core, x_hi, z, r = i // 320, i // 160 % 2, i // 80 % 2, i // 10 % 8, i % 10
    return (y * 320 + z * 40 + core * 20 + x_hi * 10 + r).astype(np.int32)


def route_kernel(ids_ref, logit_ref, out_ref):
    ids = ids_ref[...].astype(F32)
    row = lax.broadcasted_iota(jnp.int32, (TOK, TOK), 0)
    col = lax.broadcasted_iota(jnp.int32, (TOK, TOK), 1)
    ids_row = jnp.sum(jnp.where(row == col, ids, 0.0), axis=0, keepdims=True)
    rank = jnp.sum(jnp.where((ids == ids_row) & (row < col), 1.0, 0.0), axis=0, keepdims=True)
    prob = jax.nn.sigmoid(logit_ref[...]).astype(BF).astype(F32)
    out_ref[...] = jnp.concatenate([ids_row, rank, prob, jnp.zeros((5, TOK), F32)], axis=0)


def route(ids, logit):
    return pl.pallas_call(
        route_kernel,
        out_shape=jax.ShapeDtypeStruct((8, TOK), F32),
        in_specs=[VMEM, VMEM],
        out_specs=VMEM,
        name="route",
    )(ids, logit.reshape(1, TOK))


def place_kernel(where_ref, m0, m1, m2, m3, t0, t1, t2, t3, out_ref, toks, sems):
    copies = [pltpu.make_async_copy(t, toks.at[i], sems.at[i]) for i, t in enumerate((t0, t1, t2, t3))]
    for copy in copies:
        copy.start()
    core, x_hi = where_ref[0], where_ref[1]
    slot = lax.broadcasted_iota(jnp.int32, (BLOCK, TOK), 0).astype(F32)
    first = (8 * x_hi).astype(F32)
    hots = []
    for meta, other_core, other_x in ((m0, 0, 0), (m1, 1, 0), (m2, 0, 1), (m3, 1, 1)):
        src_core = core if other_core == 0 else 1 - core
        src_x = x_hi if other_x == 0 else 1 - x_hi
        base = (src_core * 20 + src_x * 10).astype(F32)
        z = meta[0:1, :] - first
        pos = jnp.where((z >= 0.0) & (z < 8.0), z * 40.0 + meta[1:2, :] + base, -1.0)
        hots.append(jnp.where(slot == pos, meta[2:3, :], 0.0).astype(BF))
    for copy in copies:
        copy.wait()
    total = None
    for i in range(2):
        hot = jnp.concatenate(hots[2 * i : 2 * i + 2], axis=1)
        pair = toks[2 * i : 2 * i + 2].reshape(2 * TOK, toks.shape[2])
        part = jnp.dot(hot, pair, preferred_element_type=F32)
        total = part if total is None else total + part
    out_ref[...] = total.astype(BF)


def place(where, metas, toks):
    width = toks[0].shape[1]
    return pl.pallas_call(
        place_kernel,
        out_shape=jax.ShapeDtypeStruct((BLOCK, width), BF),
        in_specs=[SMEM] + [VMEM] * 4 + [ANY] * 4,
        out_specs=VMEM,
        scratch_shapes=[pltpu.VMEM((4, TOK, width), BF), pltpu.SemaphoreType.DMA((4,))],
        compiler_params=pltpu.CompilerParams(vmem_limit_bytes=16 * MIB),
        cost_estimate=pl.CostEstimate(
            flops=2 * 4 * BLOCK * TOK * width, bytes_accessed=2 * width * (4 * TOK + BLOCK), transcendentals=0
        ),
        name="place",
    )(where, *metas, *toks)


def turn_kernel(where_ref, target_ref, own_ref, par_ref, out_ref, hot_ref):
    col = lax.broadcasted_iota(jnp.int32, (2 * BLOCK, 2 * BLOCK), 1)
    hot_ref[...] = jnp.where(col == target_ref[...], 1.0, 0.0).astype(BF)
    for x in range(2):
        for pair in range(2):
            for half, ref in enumerate((own_ref, par_ref)):
                runs = []
                for y in (2 * pair, 2 * pair + 1):
                    for core in range(2):
                        for x_hi in range(2):
                            same = where_ref[1] if x_hi else 1 - where_ref[1]
                            x_lo = x * same + (1 - x) * (1 - same)
                            start = ((x_lo * 4 + y) * 2 + core) * 160 + x_hi * 80
                            runs.append(ref[pl.ds(pl.multiple_of(start, 16), 80), :])
                rows = jnp.concatenate(runs, axis=0)
                turned = lax.dot_general(rows, hot_ref[...], (((0,), (0,)), ((), ())), preferred_element_type=F32)
                at = pl.ds(x * HALF // 2 + pair * 2 * BLOCK, 2 * BLOCK)
                out_ref[pl.ds(half * FD, FD), at] = turned.astype(BF)


def turn(where, target, own, par):
    return pl.pallas_call(
        turn_kernel,
        out_shape=jax.ShapeDtypeStruct((2 * FD, SLOTS), BF),
        in_specs=[SMEM] + [VMEM] * 3,
        out_specs=VMEM,
        scratch_shapes=[pltpu.VMEM((2 * BLOCK, 2 * BLOCK), BF)],
        compiler_params=pltpu.CompilerParams(vmem_limit_bytes=24 * MIB),
        cost_estimate=pl.CostEstimate(flops=2 * 2 * FD * SLOTS * 2 * BLOCK, bytes_accessed=5 * MIB, transcendentals=0),
        name="turn",
    )(where, target, own, par)


def expert_kernel(off, width, places, sides, grad, where_ref, *refs):
    n = len(places)
    pieces, (hid_ref, down_ref, par_ref), refs = refs[:n], refs[n : n + 3], refs[n + 3 :]
    outs, (rows, own_wts, sems) = refs[:-3], refs[-3:]
    core, y, x_lo = where_ref[0], where_ref[2], where_ref[3]

    def place_of(side):
        return x_lo if side == 0 else 1 - x_lo

    copies = []
    start = pl.multiple_of(core * HALF + off, 128)
    copies.append((None, pltpu.make_async_copy(down_ref.at[:, pl.ds(start, width)], own_wts, sems.at[n])))
    for i, (ref, (side, up)) in enumerate(zip(pieces, places)):
        start = pl.multiple_of(place_of(side) * QUARTER + lax.rem(y + up, 4) * BLOCK, BLOCK)
        copies.append((side, pltpu.make_async_copy(ref, rows.at[pl.ds(start, BLOCK), :], sems.at[i])))
    copies.sort(key=lambda c: c[0] in sides or c[0] is None, reverse=True)
    for _, copy in copies:
        copy.start()
    for side, copy in copies:
        if side in sides or side is None:
            copy.wait()

    tile = QUARTER // 2
    for k, side in enumerate(sides):

        @pl.loop(0, 2)
        def _(i):
            at = pl.ds(pl.multiple_of(place_of(side) * QUARTER + i * tile, 128), tile)
            total = None
            for half in range(2):
                wts = own_wts[...] if half == 0 else par_ref[:, pl.ds(off, width)]
                back = lax.dot_general(wts, rows[at, :], (((1,), (1,)), ((), ())), preferred_element_type=F32)
                part = jnp.sum(back * hid_ref[pl.ds(half * FD, FD), at].astype(F32), axis=0, keepdims=True)
                total = part if total is None else total + part
            outs[-1][k : k + 1, pl.ds(pl.multiple_of(i * tile, 128), tile)] = total

    for side, copy in copies:
        if not (side in sides or side is None):
            copy.wait()
    if grad:
        for i in range(2):
            at = pl.ds(i * FD, FD)
            outs[i][...] = jnp.dot(hid_ref[at, :], rows[...], preferred_element_type=F32).astype(BF)


def expert_part(where, pieces, hid, down, par, off, width, places, sides=(0, 1), grad=True):
    grads = (jax.ShapeDtypeStruct((FD, width), BF),) * 2 if grad else ()
    shapes = grads + (jax.ShapeDtypeStruct((len(sides), QUARTER), F32),)
    return pl.pallas_call(
        lambda *refs: expert_kernel(off, width, places, sides, grad, *refs),
        out_shape=shapes,
        in_specs=[SMEM] + [ANY] * len(pieces) + [VMEM, ANY, VMEM],
        out_specs=(VMEM,) * len(shapes),
        scratch_shapes=[
            pltpu.VMEM((SLOTS, width), BF),
            pltpu.VMEM((FD, width), BF),
            pltpu.SemaphoreType.DMA((len(pieces) + 1,)),
        ],
        compiler_params=pltpu.CompilerParams(vmem_limit_bytes=28 * MIB),
        cost_estimate=pl.CostEstimate(
            flops=2 * (len(sides) + 2 * grad) * FD * SLOTS * width,
            bytes_accessed=2 * SLOTS * (width + 2 * FD),
            transcendentals=0,
        ),
        name="expert_part",
    )(where, *pieces, hid, down, par)


def join_kernel(n, where_ref, *refs):
    own, got, out_ref, sems = refs[:n], refs[n : 2 * n], refs[2 * n], refs[2 * n + 1]
    core = where_ref[0]
    copies = []
    for refs_of, side in ((own, core), (got, 1 - core)):
        off = 0
        for ref in refs_of:
            width = ref.shape[1]
            start = pl.multiple_of(side * HALF + off, 128)
            copy = pltpu.make_async_copy(ref, out_ref.at[:, pl.ds(start, width)], sems.at[len(copies)])
            copy.start()
            copies.append(copy)
            off += width
    for copy in copies:
        copy.wait()


def join(where, own, got):
    n = len(own)
    return pl.pallas_call(
        lambda *refs: join_kernel(n, *refs),
        out_shape=jax.ShapeDtypeStruct((FD, 2 * HALF), BF),
        in_specs=[SMEM] + [ANY] * (2 * n),
        out_specs=VMEM,
        scratch_shapes=[pltpu.SemaphoreType.DMA((2 * n,))],
        compiler_params=pltpu.CompilerParams(vmem_limit_bytes=16 * MIB),
        name="join",
    )(where, *own, *got)


def tie(array, other):
    return lax.optimization_barrier((array, other))


def ring(axis, shift):
    def send(array):
        size = lax.axis_size(axis)
        return lax.ppermute(array, axis, [(i, (i + shift) % size) for i in range(size)])

    return send


def swap_x(core_too):
    axes = ("x_lo", "core", "x_hi")
    flip = 7 if core_too else 5

    def send(array):
        return lax.ppermute(array, axes, [(i, i ^ flip) for i in range(8)])

    return send


def body(out_grad, expert_ids, router_logit, hidden_saved, down_weight):
    core, x_hi = lax.axis_index("core"), lax.axis_index("x_hi")
    y, x_lo = lax.axis_index("y"), lax.axis_index("x_lo")
    where = jnp.stack([core, x_hi, y, x_lo]).astype(jnp.int32)
    swap_core, swap_xx, swap_xc = ring("core", 1), swap_x(False), swap_x(True)
    up, down, cross = ring("y", 1), ring("y", 3), ring("x_lo", 1)
    first = core == 0
    hidden = hidden_saved[0]
    down_own = down_weight[0]

    offs = [sum(CHUNKS[:k]) for k in range(len(CHUNKS))]
    n = len(CHUNKS)
    meta = route(expert_ids, router_logit)
    metas = (meta, swap_core(meta), swap_xx(meta), swap_xc(meta))
    own_tok, oth_tok = [], []
    for off, width in zip(offs, CHUNKS):
        low, high = out_grad[:, off : off + width], out_grad[:, HALF + off : HALF + off + width]
        own_tok.append(jnp.where(first, low, high))
        oth_tok.append(jnp.where(first, high, low))

    hidden_par = swap_core(hidden)
    down_par = swap_core(jnp.where(first, down_own[:, HALF:], down_own[:, :HALF]))
    target = jnp.asarray(pair_targets())
    hid = turn(where, target.reshape(2 * BLOCK, 1), hidden, hidden_par)

    def fetch(own, oth):
        return own, swap_core(oth), swap_xx(own), swap_xc(oth)

    def spread(sent):
        width = sent.shape[1]
        got = lax.all_to_all(sent.reshape(8, 40, width), "z", split_axis=0, concat_axis=0, tiled=True)
        return got.reshape(BLOCK, width)

    own, oth = own_tok[0], oth_tok[0]
    tok_0 = fetch(own, oth)
    (own, oth), tok_0 = tie((own_tok[1], oth_tok[1]), tok_0)
    tok_1 = fetch(own, oth)
    rows_0 = spread(place(where, metas, tok_0))
    sent_1, rows_0 = tie(place(where, metas, tok_1), rows_0)
    rows_1 = spread(sent_1)

    below_0, above_0, over_0 = up(rows_0), down(rows_0), cross(rows_0)
    far_0 = up(below_0)
    over_below_0, over_above_0 = up(over_0), down(over_0)
    over_far_0 = cross(far_0)
    rows, (below_0, above_0, hid) = tie(rows_1, (below_0, above_0, hid))
    over_1, above_1 = cross(rows), down(rows)
    rows, far_0 = tie(rows, far_0)
    below_1 = up(rows)
    far_1 = down(above_1)
    over_below_1, over_above_1 = up(over_1), down(over_1)
    whole = tuple((side, up_by) for side in range(2) for up_by in (0, 3, 1, 2))
    pieces = (rows_0, below_0, above_0, far_0, over_0, over_below_0, over_above_0, over_far_0)
    common = (hid, down_own, down_par)
    own_0, oth_0, score_0 = expert_part(where, pieces, *common, 0, CHUNKS[0], whole)
    far_1, score_0 = tie(far_1, score_0)
    over_far_1 = cross(far_1)
    pieces = (rows_1, below_1, above_1, far_1, over_1, over_below_1, over_above_1, over_far_1)
    (score_1,) = expert_part(where, pieces[:4], *common, CHUNKS[0], CHUNKS[1], whole[:4], sides=(0,), grad=False)
    own_1, oth_1, score_2 = expert_part(where, pieces, *common, CHUNKS[0], CHUNKS[1], whole, sides=(1,))
    weight_grad = join(where, (own_0, own_1), (swap_core(oth_0), swap_core(oth_1)))[None]

    score = (score_0 + jnp.concatenate([score_1, score_2], axis=0)).reshape(2, 4, BLOCK)
    score = jnp.where(x_lo == 0, score, score[::-1])
    spot = (target[:BLOCK, None] == jnp.arange(BLOCK, dtype=jnp.int32)[None, :]).astype(F32)
    turned = lax.dot_general(
        score.reshape(8, BLOCK), spot, (((1,), (1,)), ((), ())), precision=lax.Precision.HIGHEST,
        preferred_element_type=F32,
    ).reshape(2, 4, 2, 2, 80)
    same = (jnp.arange(2) == x_hi).reshape(1, 1, 1, 2, 1)
    parts = jnp.where(same, turned, turned[::-1]).reshape(16, 160)
    mine = lax.all_to_all(parts, ("x_lo", "y", "core"), split_axis=0, concat_axis=0, tiled=True)
    own_scores = jnp.sum(mine, axis=0).reshape(16, CAP)
    back = lax.all_to_all(own_scores, ("x_hi", "z"), split_axis=0, concat_axis=0, tiled=True)
    back, weight_grad = tie(back, weight_grad)
    slot = (meta[0] * CAP + meta[1]).astype(jnp.int32)
    hit = slot[:, None] == jnp.arange(16 * CAP, dtype=jnp.int32)[None, :]
    token_scores = jnp.sum(jnp.where(hit, back.reshape(1, 16 * CAP), 0.0), axis=1)
    prob = jax.nn.sigmoid(router_logit)
    logit_grad = prob * (1.0 - prob) / meta[2] * token_scores
    return weight_grad, logit_grad


def solution(mesh):
    fine = Mesh(mesh.devices.reshape(2, 4, 2, 2, 8), AXES)
    dp, expert = ("x_lo", "y", "core"), ("x_hi", "z")
    placed = (
        P(AXES, None),
        P(AXES, None),
        P(AXES),
        P(expert, None, dp),
        P(expert, dp, None),
    )
    return jax.shard_map(
        body,
        mesh=fine,
        in_specs=placed,
        out_specs=(P(expert, dp, None), P(AXES)),
        check_vma=False,
    )
```

```python
import jax
import jax.numpy as jnp
import numpy as np
from jax import lax
from jax.experimental import pallas as pl
from jax.experimental.pallas import tpu as pltpu
from jax.sharding import Mesh, PartitionSpec as P

BF = jnp.bfloat16
F32 = jnp.float32
CAP = 10
TOK = 128
CHUNKS = (1280, 1280)
HALF = 2560
FD = 256
BLOCK = 320
QUARTER = 1280
TOP = 160
SLOTS = 2560
MIB = 1 << 20
AXES = ("x_lo", "y", "core", "x_hi", "z")
VMEM = pl.BlockSpec(memory_space=pltpu.VMEM)
SMEM = pl.BlockSpec(memory_space=pltpu.SMEM)
ANY = pl.BlockSpec(memory_space=pl.ANY)


def pair_targets():
    i = np.arange(2 * BLOCK)
    y, core, x_hi, z, r = i // 320, i // 160 % 2, i // 80 % 2, i // 10 % 8, i % 10
    return (y * 320 + z * 40 + core * 20 + x_hi * 10 + r).astype(np.int32)


def route_kernel(ids_ref, logit_ref, out_ref):
    ids = ids_ref[...].astype(F32)
    row = lax.broadcasted_iota(jnp.int32, (TOK, TOK), 0)
    col = lax.broadcasted_iota(jnp.int32, (TOK, TOK), 1)
    ids_row = jnp.sum(jnp.where(row == col, ids, 0.0), axis=0, keepdims=True)
    rank = jnp.sum(jnp.where((ids == ids_row) & (row < col), 1.0, 0.0), axis=0, keepdims=True)
    prob = jax.nn.sigmoid(logit_ref[...]).astype(BF).astype(F32)
    out_ref[...] = jnp.concatenate([ids_row, rank, prob, jnp.zeros((5, TOK), F32)], axis=0)


def route(ids, logit):
    return pl.pallas_call(
        route_kernel,
        out_shape=jax.ShapeDtypeStruct((8, TOK), F32),
        in_specs=[VMEM, VMEM],
        out_specs=VMEM,
        name="route",
    )(ids, logit.reshape(1, TOK))


def place_kernel(where_ref, m0, m1, m2, m3, t0, t1, t2, t3, out_ref, toks, sems):
    copies = [pltpu.make_async_copy(t, toks.at[i], sems.at[i]) for i, t in enumerate((t0, t1, t2, t3))]
    for copy in copies:
        copy.start()
    core, x_hi = where_ref[0], where_ref[1]
    slot = lax.broadcasted_iota(jnp.int32, (BLOCK, TOK), 0).astype(F32)
    first = (8 * x_hi).astype(F32)
    hots = []
    for meta, other_core, other_x in ((m0, 0, 0), (m1, 1, 0), (m2, 0, 1), (m3, 1, 1)):
        src_core = core if other_core == 0 else 1 - core
        src_x = x_hi if other_x == 0 else 1 - x_hi
        base = (src_core * 20 + src_x * 10).astype(F32)
        z = meta[0:1, :] - first
        pos = jnp.where((z >= 0.0) & (z < 8.0), z * 40.0 + meta[1:2, :] + base, -1.0)
        hots.append(jnp.where(slot == pos, meta[2:3, :], 0.0).astype(BF))
    for copy in copies:
        copy.wait()
    total = None
    for i in range(2):
        hot = jnp.concatenate(hots[2 * i : 2 * i + 2], axis=1)
        pair = toks[2 * i : 2 * i + 2].reshape(2 * TOK, toks.shape[2])
        part = jnp.dot(hot, pair, preferred_element_type=F32)
        total = part if total is None else total + part
    out_ref[...] = total.astype(BF)


def place(where, metas, toks):
    width = toks[0].shape[1]
    return pl.pallas_call(
        place_kernel,
        out_shape=jax.ShapeDtypeStruct((BLOCK, width), BF),
        in_specs=[SMEM] + [VMEM] * 4 + [ANY] * 4,
        out_specs=VMEM,
        scratch_shapes=[pltpu.VMEM((4, TOK, width), BF), pltpu.SemaphoreType.DMA((4,))],
        compiler_params=pltpu.CompilerParams(vmem_limit_bytes=16 * MIB),
        cost_estimate=pl.CostEstimate(
            flops=2 * 4 * BLOCK * TOK * width, bytes_accessed=2 * width * (4 * TOK + BLOCK), transcendentals=0
        ),
        name="place",
    )(where, *metas, *toks)


def turn_kernel(where_ref, target_ref, own_ref, par_ref, out_ref, hot_ref):
    col = lax.broadcasted_iota(jnp.int32, (2 * BLOCK, 2 * BLOCK), 1)
    hot_ref[...] = jnp.where(col == target_ref[...], 1.0, 0.0).astype(BF)
    for x in range(2):
        for pair in range(2):
            for half, ref in enumerate((own_ref, par_ref)):
                runs = []
                for y in (2 * pair, 2 * pair + 1):
                    for core in range(2):
                        for x_hi in range(2):
                            same = where_ref[1] if x_hi else 1 - where_ref[1]
                            x_lo = x * same + (1 - x) * (1 - same)
                            start = ((x_lo * 4 + y) * 2 + core) * 160 + x_hi * 80
                            runs.append(ref[pl.ds(pl.multiple_of(start, 16), 80), :])
                rows = jnp.concatenate(runs, axis=0)
                turned = lax.dot_general(rows, hot_ref[...], (((0,), (0,)), ((), ())), preferred_element_type=F32)
                at = pl.ds(x * HALF // 2 + pair * 2 * BLOCK, 2 * BLOCK)
                out_ref[pl.ds(half * FD, FD), at] = turned.astype(BF)


def turn(where, target, own, par):
    return pl.pallas_call(
        turn_kernel,
        out_shape=jax.ShapeDtypeStruct((2 * FD, SLOTS), BF),
        in_specs=[SMEM] + [VMEM] * 3,
        out_specs=VMEM,
        scratch_shapes=[pltpu.VMEM((2 * BLOCK, 2 * BLOCK), BF)],
        compiler_params=pltpu.CompilerParams(vmem_limit_bytes=24 * MIB),
        cost_estimate=pl.CostEstimate(flops=2 * 2 * FD * SLOTS * 2 * BLOCK, bytes_accessed=5 * MIB, transcendentals=0),
        name="turn",
    )(where, target, own, par)


def expert_kernel(off, width, places, sides, grad, where_ref, *refs):
    n = len(places)
    pieces, (hid_ref, down_ref, par_ref), refs = refs[:n], refs[n : n + 3], refs[n + 3 :]
    outs, (rows, wts, sems) = refs[:-3], refs[-3:]
    core, y, x_lo = where_ref[0], where_ref[2], where_ref[3]

    def place_of(side):
        return x_lo if side == 0 else 1 - x_lo

    start = pl.multiple_of(core * HALF + off, 128)
    down = down_ref.at[:, pl.ds(start, width)]
    par = par_ref.at[:, pl.ds(off, width)]
    copies = [
        pltpu.make_async_copy(down, wts.at[pl.ds(0, FD), :], sems.at[0]),
        pltpu.make_async_copy(par, wts.at[pl.ds(FD, FD), :], sems.at[1]),
    ]
    for copy in copies:
        copy.start()
    for ref, (side, up) in zip(pieces, places):
        start = pl.multiple_of(place_of(side) * QUARTER + lax.rem(y + up, 4) * BLOCK, BLOCK)
        rows[pl.ds(start, BLOCK), :] = ref[...]
    for copy in copies:
        copy.wait()

    tile = QUARTER // 2
    for k, side in enumerate(sides):
        for i in range(2):
            at = pl.ds(pl.multiple_of(place_of(side) * QUARTER + i * tile, 128), tile)
            back = lax.dot_general(wts[...], rows[at, :], (((1,), (1,)), ((), ())), preferred_element_type=F32)
            part = jnp.sum(back * hid_ref[:, at].astype(F32), axis=0, keepdims=True)
            outs[-1][k : k + 1, pl.ds(i * tile, tile)] = part

    if grad:
        total = jnp.dot(hid_ref[...], rows[...], preferred_element_type=F32).astype(BF)
        outs[0][...] = total[:FD]
        outs[1][...] = total[FD:]


def expert_part(where, pieces, hid, down, par, off, width, places, sides=(0, 1), grad=True):
    grads = (jax.ShapeDtypeStruct((FD, width), BF),) * 2 if grad else ()
    shapes = grads + (jax.ShapeDtypeStruct((len(sides), QUARTER), F32),)
    return pl.pallas_call(
        lambda *refs: expert_kernel(off, width, places, sides, grad, *refs),
        out_shape=shapes,
        in_specs=[SMEM] + [VMEM] * len(pieces) + [VMEM, ANY, ANY],
        out_specs=(VMEM,) * len(shapes),
        scratch_shapes=[
            pltpu.VMEM((SLOTS, width), BF),
            pltpu.VMEM((2 * FD, width), BF),
            pltpu.SemaphoreType.DMA((2,)),
        ],
        compiler_params=pltpu.CompilerParams(vmem_limit_bytes=28 * MIB),
        cost_estimate=pl.CostEstimate(
            flops=0,
            bytes_accessed=0,
            transcendentals=0,
        ),
        name="expert_part",
    )(where, *pieces, hid, down, par)


def join_kernel(n, where_ref, *refs):
    own, got, out_ref, sems = refs[:n], refs[n : 2 * n], refs[2 * n], refs[2 * n + 1]
    core = where_ref[0]
    copies = []
    for refs_of, side in ((own, core), (got, 1 - core)):
        off = 0
        for ref in refs_of:
            width = ref.shape[1]
            start = pl.multiple_of(side * HALF + off, 128)
            copy = pltpu.make_async_copy(ref, out_ref.at[:, pl.ds(start, width)], sems.at[len(copies)])
            copy.start()
            copies.append(copy)
            off += width
    for copy in copies:
        copy.wait()


def join(where, own, got):
    n = len(own)
    return pl.pallas_call(
        lambda *refs: join_kernel(n, *refs),
        out_shape=jax.ShapeDtypeStruct((FD, 2 * HALF), BF),
        in_specs=[SMEM] + [ANY] * (2 * n),
        out_specs=VMEM,
        scratch_shapes=[pltpu.SemaphoreType.DMA((2 * n,))],
        compiler_params=pltpu.CompilerParams(vmem_limit_bytes=16 * MIB),
        name="join",
    )(where, *own, *got)


def tie(array, other):
    return lax.optimization_barrier((array, other))


def ring(axis, shift):
    def send(array):
        size = lax.axis_size(axis)
        return lax.ppermute(array, axis, [(i, (i + shift) % size) for i in range(size)])

    return send


def swap_x(core_too):
    axes = ("x_lo", "core", "x_hi")
    flip = 7 if core_too else 5

    def send(array):
        return lax.ppermute(array, axes, [(i, i ^ flip) for i in range(8)])

    return send


def body(out_grad, expert_ids, router_logit, hidden_saved, down_weight):
    core, x_hi = lax.axis_index("core"), lax.axis_index("x_hi")
    y, x_lo = lax.axis_index("y"), lax.axis_index("x_lo")
    where = jnp.stack([core, x_hi, y, x_lo]).astype(jnp.int32)
    swap_core, swap_xx, swap_xc = ring("core", 1), swap_x(False), swap_x(True)
    up, down, cross = ring("y", 1), ring("y", 3), ring("x_lo", 1)
    first = core == 0
    hidden = hidden_saved[0]
    down_own = down_weight[0]

    offs = [sum(CHUNKS[:k]) for k in range(len(CHUNKS))]
    n = len(CHUNKS)
    meta = route(expert_ids, router_logit)
    metas = (meta, swap_core(meta), swap_xx(meta), swap_xc(meta))
    own_tok, oth_tok = [], []
    for off, width in zip(offs, CHUNKS):
        low, high = out_grad[:, off : off + width], out_grad[:, HALF + off : HALF + off + width]
        own_tok.append(jnp.where(first, low, high))
        oth_tok.append(jnp.where(first, high, low))

    hidden_par = swap_core(hidden)
    down_par = swap_core(jnp.where(first, down_own[:, HALF:], down_own[:, :HALF]))
    target = jnp.asarray(pair_targets())
    hid = turn(where, target.reshape(2 * BLOCK, 1), hidden, hidden_par)

    def fetch(own, oth):
        return own, swap_core(oth), swap_xx(own), swap_xc(oth)

    def spread(sent):
        width = sent.shape[1]
        got = lax.all_to_all(sent.reshape(8, 40, width), "z", split_axis=0, concat_axis=0, tiled=True)
        return got.reshape(BLOCK, width)

    own, oth = own_tok[0], oth_tok[0]
    tok_0 = fetch(own, oth)
    (own, oth), tok_0 = tie((own_tok[1], oth_tok[1]), tok_0)
    tok_1 = fetch(own, oth)
    rows_0 = spread(place(where, metas, tok_0))
    sent_1, rows_0 = tie(place(where, metas, tok_1), rows_0)
    rows_1 = spread(sent_1)

    below_0, above_0, over_0 = up(rows_0), down(rows_0), cross(rows_0)
    below_0, hid = tie(below_0, hid)
    far_0 = up(below_0)
    over_below_0, over_above_0 = up(over_0), down(over_0)
    over_far_0 = cross(far_0)
    rows, (below_0, above_0) = tie(rows_1, (below_0, above_0))
    over_1, above_1 = cross(rows), down(rows)
    rows, far_0 = tie(rows, far_0)
    below_1 = up(rows)
    far_1 = down(above_1)
    over_below_1, over_above_1 = up(over_1), down(over_1)
    whole = tuple((side, up_by) for side in range(2) for up_by in (0, 3, 1, 2))
    pieces = (rows_0, below_0, above_0, far_0, over_0, over_below_0, over_above_0, over_far_0)
    common = (hid, down_own, down_par)
    own_0, oth_0, score_0 = expert_part(where, pieces, *common, 0, CHUNKS[0], whole)
    far_1, score_0 = tie(far_1, score_0)
    over_far_1 = cross(far_1)
    pieces = (rows_1, below_1, above_1, far_1, over_1, over_below_1, over_above_1, over_far_1)
    (score_1,) = expert_part(where, pieces[:4], *common, CHUNKS[0], CHUNKS[1], whole[:4], sides=(0,), grad=False)
    own_1, oth_1, score_2 = expert_part(where, pieces, *common, CHUNKS[0], CHUNKS[1], whole, sides=(1,))
    weight_grad = join(where, (own_0, own_1), (swap_core(oth_0), swap_core(oth_1)))[None]

    score = (score_0 + jnp.concatenate([score_1, score_2], axis=0)).reshape(2, 4, BLOCK)
    score = jnp.where(x_lo == 0, score, score[::-1])
    spot = (target[:BLOCK, None] == jnp.arange(BLOCK, dtype=jnp.int32)[None, :]).astype(F32)
    turned = lax.dot_general(
        score.reshape(8, BLOCK), spot, (((1,), (1,)), ((), ())), precision=lax.Precision.HIGHEST,
        preferred_element_type=F32,
    ).reshape(2, 4, 2, 2, 80)
    same = (jnp.arange(2) == x_hi).reshape(1, 1, 1, 2, 1)
    parts = jnp.where(same, turned, turned[::-1]).reshape(16, 160)
    mine = lax.all_to_all(parts, ("x_lo", "y", "core"), split_axis=0, concat_axis=0, tiled=True)
    own_scores = jnp.sum(mine, axis=0).reshape(16, CAP)
    back = lax.all_to_all(own_scores, ("x_hi", "z"), split_axis=0, concat_axis=0, tiled=True)
    back, weight_grad = tie(back, weight_grad)
    slot = (meta[0] * CAP + meta[1]).astype(jnp.int32)
    hit = slot[:, None] == jnp.arange(16 * CAP, dtype=jnp.int32)[None, :]
    token_scores = jnp.sum(jnp.where(hit, back.reshape(1, 16 * CAP), 0.0), axis=1)
    prob = jax.nn.sigmoid(router_logit)
    logit_grad = prob * (1.0 - prob) / meta[2] * token_scores
    return weight_grad, logit_grad


def solution(mesh):
    fine = Mesh(mesh.devices.reshape(2, 4, 2, 2, 8), AXES)
    dp, expert = ("x_lo", "y", "core"), ("x_hi", "z")
    placed = (
        P(AXES, None),
        P(AXES, None),
        P(AXES),
        P(expert, None, dp),
        P(expert, dp, None),
    )
    return jax.shard_map(
        body,
        mesh=fine,
        in_specs=placed,
        out_specs=(P(expert, dp, None), P(AXES)),
        check_vma=False,
    )
```

```python
import jax
import jax.numpy as jnp
import numpy as np
from jax import lax
from jax.experimental import pallas as pl
from jax.experimental.pallas import tpu as pltpu
from jax.sharding import Mesh, PartitionSpec as P

BF = jnp.bfloat16
F32 = jnp.float32
CAP = 10
TOK = 128
CHUNKS = (1280, 1280)
HALF = 2560
FD = 256
BLOCK = 320
QUARTER = 1280
TOP = 160
SLOTS = 2560
MIB = 1 << 20
AXES = ("x_lo", "y", "core", "x_hi", "z")
VMEM = pl.BlockSpec(memory_space=pltpu.VMEM)
SMEM = pl.BlockSpec(memory_space=pltpu.SMEM)
ANY = pl.BlockSpec(memory_space=pl.ANY)


def pair_targets():
    i = np.arange(2 * BLOCK)
    y, core, x_hi, z, r = i // 320, i // 160 % 2, i // 80 % 2, i // 10 % 8, i % 10
    return (y * 320 + z * 40 + core * 20 + x_hi * 10 + r).astype(np.int32)


def route_kernel(ids_ref, logit_ref, out_ref):
    ids = ids_ref[...].astype(F32)
    row = lax.broadcasted_iota(jnp.int32, (TOK, TOK), 0)
    col = lax.broadcasted_iota(jnp.int32, (TOK, TOK), 1)
    ids_row = jnp.sum(jnp.where(row == col, ids, 0.0), axis=0, keepdims=True)
    rank = jnp.sum(jnp.where((ids == ids_row) & (row < col), 1.0, 0.0), axis=0, keepdims=True)
    prob = jax.nn.sigmoid(logit_ref[...]).astype(BF).astype(F32)
    out_ref[...] = jnp.concatenate([ids_row, rank, prob, jnp.zeros((5, TOK), F32)], axis=0)


def route(ids, logit):
    return pl.pallas_call(
        route_kernel,
        out_shape=jax.ShapeDtypeStruct((8, TOK), F32),
        in_specs=[VMEM, VMEM],
        out_specs=VMEM,
        name="route",
    )(ids, logit.reshape(1, TOK))


def place_kernel(where_ref, m0, m1, m2, m3, t0, t1, t2, t3, out_ref):
    core, x_hi = where_ref[0], where_ref[1]
    slot = lax.broadcasted_iota(jnp.int32, (BLOCK, TOK), 0).astype(F32)
    first = (8 * x_hi).astype(F32)
    hots = []
    for meta, other_core, other_x in ((m0, 0, 0), (m1, 1, 0), (m2, 0, 1), (m3, 1, 1)):
        src_core = core if other_core == 0 else 1 - core
        src_x = x_hi if other_x == 0 else 1 - x_hi
        base = (src_core * 20 + src_x * 10).astype(F32)
        z = meta[0:1, :] - first
        pos = jnp.where((z >= 0.0) & (z < 8.0), z * 40.0 + meta[1:2, :] + base, -1.0)
        hots.append(jnp.where(slot == pos, meta[2:3, :], 0.0).astype(BF))
    total = None
    for i, (low, high) in enumerate(((t0, t1), (t2, t3))):
        hot = jnp.concatenate(hots[2 * i : 2 * i + 2], axis=1)
        pair = jnp.concatenate([low[...], high[...]], axis=0)
        part = jnp.dot(hot, pair, preferred_element_type=F32)
        total = part if total is None else total + part
    out_ref[...] = total.astype(BF)


def place(where, metas, toks):
    width = toks[0].shape[1]
    return pl.pallas_call(
        place_kernel,
        out_shape=jax.ShapeDtypeStruct((BLOCK, width), BF),
        in_specs=[SMEM] + [VMEM] * 8,
        out_specs=VMEM,
        compiler_params=pltpu.CompilerParams(vmem_limit_bytes=16 * MIB),
        cost_estimate=pl.CostEstimate(
            flops=2 * 4 * BLOCK * TOK * width, bytes_accessed=2 * width * (4 * TOK + BLOCK), transcendentals=0
        ),
        name="place",
    )(where, *metas, *toks)


def turn_kernel(where_ref, target_ref, own_ref, par_ref, out_ref, hot_ref):
    col = lax.broadcasted_iota(jnp.int32, (2 * BLOCK, 2 * BLOCK), 1)
    hot_ref[...] = jnp.where(col == target_ref[...], 1.0, 0.0).astype(BF)
    for x in range(2):
        for pair in range(2):
            for half, ref in enumerate((own_ref, par_ref)):
                runs = []
                for y in (2 * pair, 2 * pair + 1):
                    for core in range(2):
                        for x_hi in range(2):
                            same = where_ref[1] if x_hi else 1 - where_ref[1]
                            x_lo = x * same + (1 - x) * (1 - same)
                            start = ((x_lo * 4 + y) * 2 + core) * 160 + x_hi * 80
                            runs.append(ref[pl.ds(pl.multiple_of(start, 16), 80), :])
                rows = jnp.concatenate(runs, axis=0)
                turned = lax.dot_general(rows, hot_ref[...], (((0,), (0,)), ((), ())), preferred_element_type=F32)
                at = pl.ds(x * HALF // 2 + pair * 2 * BLOCK, 2 * BLOCK)
                out_ref[pl.ds(half * FD, FD), at] = turned.astype(BF)


def turn(where, target, own, par):
    return pl.pallas_call(
        turn_kernel,
        out_shape=jax.ShapeDtypeStruct((2 * FD, SLOTS), BF),
        in_specs=[SMEM] + [VMEM] * 3,
        out_specs=VMEM,
        scratch_shapes=[pltpu.VMEM((2 * BLOCK, 2 * BLOCK), BF)],
        compiler_params=pltpu.CompilerParams(vmem_limit_bytes=24 * MIB),
        cost_estimate=pl.CostEstimate(flops=2 * 2 * FD * SLOTS * 2 * BLOCK, bytes_accessed=5 * MIB, transcendentals=0),
        name="turn",
    )(where, target, own, par)


def expert_kernel(off, width, places, sides, grad, where_ref, *refs):
    n = len(places)
    pieces, (hid_ref, down_ref, par_ref), refs = refs[:n], refs[n : n + 3], refs[n + 3 :]
    outs, (rows, wts, sems) = refs[:-3], refs[-3:]
    core, y, x_lo = where_ref[0], where_ref[2], where_ref[3]

    def place_of(side):
        return x_lo if side == 0 else 1 - x_lo

    start = pl.multiple_of(core * HALF + off, 128)
    down = down_ref.at[:, pl.ds(start, width)]
    par = par_ref.at[:, pl.ds(off, width)]
    copies = [
        pltpu.make_async_copy(down, wts.at[pl.ds(0, FD), :], sems.at[0]),
        pltpu.make_async_copy(par, wts.at[pl.ds(FD, FD), :], sems.at[1]),
    ]
    for copy in copies:
        copy.start()
    for ref, (side, up) in zip(pieces, places):
        start = pl.multiple_of(place_of(side) * QUARTER + lax.rem(y + up, 4) * BLOCK, BLOCK)
        rows[pl.ds(start, BLOCK), :] = ref[...]
    for copy in copies:
        copy.wait()

    tile = QUARTER // 2
    for k, side in enumerate(sides):
        for i in range(2):
            at = pl.ds(pl.multiple_of(place_of(side) * QUARTER + i * tile, 128), tile)
            back = lax.dot_general(wts[...], rows[at, :], (((1,), (1,)), ((), ())), preferred_element_type=F32)
            part = jnp.sum(back * hid_ref[:, at].astype(F32), axis=0, keepdims=True)
            outs[-1][k : k + 1, pl.ds(i * tile, tile)] = part

    if grad:
        total = jnp.dot(hid_ref[...], rows[...], preferred_element_type=F32).astype(BF)
        outs[0][...] = total[:FD]
        outs[1][...] = total[FD:]


def expert_part(where, pieces, hid, down, par, off, width, places, sides=(0, 1), grad=True):
    grads = (jax.ShapeDtypeStruct((FD, width), BF),) * 2 if grad else ()
    shapes = grads + (jax.ShapeDtypeStruct((len(sides), QUARTER), F32),)
    return pl.pallas_call(
        lambda *refs: expert_kernel(off, width, places, sides, grad, *refs),
        out_shape=shapes,
        in_specs=[SMEM] + [VMEM] * len(pieces) + [VMEM, ANY, ANY],
        out_specs=(VMEM,) * len(shapes),
        scratch_shapes=[
            pltpu.VMEM((SLOTS, width), BF),
            pltpu.VMEM((2 * FD, width), BF),
            pltpu.SemaphoreType.DMA((2,)),
        ],
        compiler_params=pltpu.CompilerParams(vmem_limit_bytes=28 * MIB),
        cost_estimate=pl.CostEstimate(
            flops=0,
            bytes_accessed=0,
            transcendentals=0,
        ),
        name="expert_part",
    )(where, *pieces, hid, down, par)


def join_kernel(n, where_ref, *refs):
    own, got, out_ref, sems = refs[:n], refs[n : 2 * n], refs[2 * n], refs[2 * n + 1]
    core = where_ref[0]
    copies = []
    for refs_of, side in ((own, core), (got, 1 - core)):
        off = 0
        for ref in refs_of:
            width = ref.shape[1]
            start = pl.multiple_of(side * HALF + off, 128)
            copy = pltpu.make_async_copy(ref, out_ref.at[:, pl.ds(start, width)], sems.at[len(copies)])
            copy.start()
            copies.append(copy)
            off += width
    for copy in copies:
        copy.wait()


def join(where, own, got):
    n = len(own)
    return pl.pallas_call(
        lambda *refs: join_kernel(n, *refs),
        out_shape=jax.ShapeDtypeStruct((FD, 2 * HALF), BF),
        in_specs=[SMEM] + [ANY] * (2 * n),
        out_specs=VMEM,
        scratch_shapes=[pltpu.SemaphoreType.DMA((2 * n,))],
        compiler_params=pltpu.CompilerParams(vmem_limit_bytes=16 * MIB),
        name="join",
    )(where, *own, *got)


def tie(array, other):
    return lax.optimization_barrier((array, other))


def ring(axis, shift):
    def send(array):
        size = lax.axis_size(axis)
        return lax.ppermute(array, axis, [(i, (i + shift) % size) for i in range(size)])

    return send


def swap_x(core_too):
    axes = ("x_lo", "core", "x_hi")
    flip = 7 if core_too else 5

    def send(array):
        return lax.ppermute(array, axes, [(i, i ^ flip) for i in range(8)])

    return send


def body(out_grad, expert_ids, router_logit, hidden_saved, down_weight):
    core, x_hi = lax.axis_index("core"), lax.axis_index("x_hi")
    y, x_lo = lax.axis_index("y"), lax.axis_index("x_lo")
    where = jnp.stack([core, x_hi, y, x_lo]).astype(jnp.int32)
    swap_core, swap_xx, swap_xc = ring("core", 1), swap_x(False), swap_x(True)
    up, down, cross = ring("y", 1), ring("y", 3), ring("x_lo", 1)
    first = core == 0
    hidden = hidden_saved[0]
    down_own = down_weight[0]

    offs = [sum(CHUNKS[:k]) for k in range(len(CHUNKS))]
    n = len(CHUNKS)
    meta = route(expert_ids, router_logit)
    metas = (meta, swap_core(meta), swap_xx(meta), swap_xc(meta))
    own_tok, oth_tok = [], []
    for off, width in zip(offs, CHUNKS):
        low, high = out_grad[:, off : off + width], out_grad[:, HALF + off : HALF + off + width]
        own_tok.append(jnp.where(first, low, high))
        oth_tok.append(jnp.where(first, high, low))

    hidden_par = swap_core(hidden)
    down_par = swap_core(jnp.where(first, down_own[:, HALF:], down_own[:, :HALF]))
    target = jnp.asarray(pair_targets())
    hid = turn(where, target.reshape(2 * BLOCK, 1), hidden, hidden_par)

    def fetch(own, oth):
        return own, swap_core(oth), swap_xx(own), swap_xc(oth)

    def spread(sent):
        width = sent.shape[1]
        got = lax.all_to_all(sent.reshape(8, 40, width), "z", split_axis=0, concat_axis=0, tiled=True)
        return got.reshape(BLOCK, width)

    own, oth = own_tok[0], oth_tok[0]
    tok_0 = fetch(own, oth)
    (own, oth), tok_0 = tie((own_tok[1], oth_tok[1]), tok_0)
    tok_1 = fetch(own, oth)
    rows_0 = spread(place(where, metas, tok_0))
    sent_1, rows_0 = tie(place(where, metas, tok_1), rows_0)
    rows_1 = spread(sent_1)

    below_0, above_0, over_0 = up(rows_0), down(rows_0), cross(rows_0)
    below_0, hid = tie(below_0, hid)
    far_0 = up(below_0)
    over_below_0, over_above_0 = up(over_0), down(over_0)
    over_far_0 = cross(far_0)
    rows, (below_0, above_0) = tie(rows_1, (below_0, above_0))
    over_1, above_1 = cross(rows), down(rows)
    rows, far_0 = tie(rows, far_0)
    below_1 = up(rows)
    far_1 = down(above_1)
    over_below_1, over_above_1 = up(over_1), down(over_1)
    whole = tuple((side, up_by) for side in range(2) for up_by in (0, 3, 1, 2))
    pieces = (rows_0, below_0, above_0, far_0, over_0, over_below_0, over_above_0, over_far_0)
    common = (hid, down_own, down_par)
    own_0, oth_0, score_0 = expert_part(where, pieces, *common, 0, CHUNKS[0], whole)
    far_1, score_0 = tie(far_1, score_0)
    over_far_1 = cross(far_1)
    pieces = (rows_1, below_1, above_1, far_1, over_1, over_below_1, over_above_1, over_far_1)
    (score_1,) = expert_part(where, pieces[:4], *common, CHUNKS[0], CHUNKS[1], whole[:4], sides=(0,), grad=False)
    own_1, oth_1, score_2 = expert_part(where, pieces, *common, CHUNKS[0], CHUNKS[1], whole, sides=(1,))
    weight_grad = join(where, (own_0, own_1), (swap_core(oth_0), swap_core(oth_1)))[None]

    score = (score_0 + jnp.concatenate([score_1, score_2], axis=0)).reshape(2, 4, BLOCK)
    score = jnp.where(x_lo == 0, score, score[::-1])
    spot = (target[:BLOCK, None] == jnp.arange(BLOCK, dtype=jnp.int32)[None, :]).astype(F32)
    turned = lax.dot_general(
        score.reshape(8, BLOCK), spot, (((1,), (1,)), ((), ())), precision=lax.Precision.HIGHEST,
        preferred_element_type=F32,
    ).reshape(2, 4, 2, 2, 80)
    same = (jnp.arange(2) == x_hi).reshape(1, 1, 1, 2, 1)
    parts = jnp.where(same, turned, turned[::-1]).reshape(16, 160)
    mine = lax.all_to_all(parts, ("x_lo", "y", "core"), split_axis=0, concat_axis=0, tiled=True)
    own_scores = jnp.sum(mine, axis=0).reshape(16, CAP)
    back = lax.all_to_all(own_scores, ("x_hi", "z"), split_axis=0, concat_axis=0, tiled=True)
    back, weight_grad = tie(back, weight_grad)
    slot = (meta[0] * CAP + meta[1]).astype(jnp.int32)
    hit = slot[:, None] == jnp.arange(16 * CAP, dtype=jnp.int32)[None, :]
    token_scores = jnp.sum(jnp.where(hit, back.reshape(1, 16 * CAP), 0.0), axis=1)
    prob = jax.nn.sigmoid(router_logit)
    logit_grad = prob * (1.0 - prob) / meta[2] * token_scores
    return weight_grad, logit_grad


def solution(mesh):
    fine = Mesh(mesh.devices.reshape(2, 4, 2, 2, 8), AXES)
    dp, expert = ("x_lo", "y", "core"), ("x_hi", "z")
    placed = (
        P(AXES, None),
        P(AXES, None),
        P(AXES),
        P(expert, None, dp),
        P(expert, dp, None),
    )
    return jax.shard_map(
        body,
        mesh=fine,
        in_specs=placed,
        out_specs=(P(expert, dp, None), P(AXES)),
        check_vma=False,
    )
```
